32 devices in a mesh: src: 4 (over z), ctx: 8 (over y, x, core).
Axes of the slice: x: 2, y: 2, z: 4, core: 2. Of those that a mesh axis runs over, the one named last changes fastest.
Arguments:
- embeddings: bfloat16 [32768, 1536], P(('src', 'ctx')), may hold values from -6 to 6
- positions: int32 [32768], P(('src', 'ctx')), may hold values from -1 to 16383, as said below
- in_weight: bfloat16 [1536, 768], replicated, may hold values from -0.15625 to 0.15625
- norm_gain: float32 [768], replicated, may hold values from 0.1 to 1.9
- qkv_weight: bfloat16 [768, 3, 768], P(None, None, 'src'), may hold values from -3 to 3
- out_weight: bfloat16 [768, 768], P('src'), may hold values from -0.875 to 0.875
- neighbors: int32 [128, 4], replicated, may hold values from 0 to 127, as said below
- upstream: bfloat16 [16384, 768], P('ctx'), may hold values from -0.125 to 0.125
Outputs:
- encoded: bfloat16 [16384, 768], P('ctx')
- in_grad: float32 [1536, 768], P('ctx', 'src')
- gain_grad: float32 [768], replicated
- qkv_grad: float32 [768, 3, 768], P(None, None, 'src')
- out_grad: float32 [768, 768], P('src')
The draws below stay inside these ranges and needn't reach their ends.
Inputs may be any that keep to these rules, and one draw needn't show every extreme that they name: Every position 0 to 16383 belongs to exactly one tile; -1 marks a dropped tile. The 1024 tiles of one producer device (consecutive rows) send at most 128 kept tiles to one sequence shard (positions 2048 s to 2048 s + 2047), and every shard receives exactly 128 from some producer device. neighbors[b, 0] = b; entry 1 is a block of b's own shard of 16 consecutive blocks; entry 2 a block of the shard before (of its own for the first shard); entry 3 a block of the shard after (of its own for the last). Entries may repeat.
All inputs are finite; a program needn't handle non-finite values.
Results may differ from the reference program's by a relative error of at most 0.018.
Values may be sent and summed in bfloat16 or wider, within the bound.
A program may use at most 192 MiB of HBM per device.

```python
import jax
import jax.numpy as jnp
from jax import lax

D = 768
EMB = 1536
HEAD = 48
BLOCK = 128
NBR = 4
SEQ_DEV = 2048
HEAD_GROUPS = 4
CAP = 128
PROD_DEV = 1024
TILES = 32768
SEQ = 16384
NBLK = 128


def draw_positions(key, part):
    key = jax.random.fold_in(key, 11)
    producers = TILES // PROD_DEV
    shards = PROD_DEV // CAP
    pair_key, share_key, order_key, shuffle_key = jax.random.split(key, 4)
    pairing = jax.vmap(lambda subkey: jax.random.permutation(subkey, producers))(jax.random.split(pair_key, shards))
    shares = jax.random.randint(share_key, (shards, producers // 2), 0, CAP + 1)
    shares = shares.at[:, 0].set(CAP)
    pair_counts = jnp.stack([shares, CAP - shares], axis=2).reshape(shards, producers)
    counts = jnp.zeros((shards, producers), jnp.int32).at[jnp.arange(shards)[:, None], pairing].set(pair_counts)
    orders = jax.vmap(lambda subkey: jax.random.permutation(subkey, SEQ_DEV))(jax.random.split(order_key, shards))
    starts = jnp.cumsum(counts, axis=1) - counts
    within = jnp.arange(CAP)
    lookup = jnp.minimum(starts[:, :, None] + within[None, None, :], SEQ_DEV - 1)
    picked = jnp.take_along_axis(orders, lookup.reshape(shards, producers * CAP), axis=1)
    picked = picked.reshape(shards, producers, CAP)
    placed = picked + (jnp.arange(shards) * SEQ_DEV)[:, None, None]
    placed = jnp.where(within[None, None, :] < counts[:, :, None], placed, -1)
    tile_rows = jnp.transpose(placed, (1, 0, 2)).reshape(producers, shards * CAP)
    shuffle = jax.vmap(lambda subkey: jax.random.permutation(subkey, shards * CAP))(jax.random.split(shuffle_key, producers))
    tile_rows = jnp.take_along_axis(tile_rows, shuffle, axis=1)
    return tile_rows.reshape(-1).astype(jnp.int32)


def draw_neighbors(key, part):
    key = jax.random.fold_in(key, 23)
    per_shard = SEQ_DEV // BLOCK
    shards = NBLK // per_shard
    inside_key, earlier_key, further_key = jax.random.split(key, 3)
    blocks = jnp.arange(NBLK)
    home_shard = blocks // per_shard
    inside = home_shard * per_shard + jax.random.randint(inside_key, (NBLK,), 0, per_shard)
    earlier = jnp.maximum(home_shard - 1, 0) * per_shard + jax.random.randint(earlier_key, (NBLK,), 0, per_shard)
    further = jnp.minimum(home_shard + 1, shards - 1) * per_shard + jax.random.randint(further_key, (NBLK,), 0, per_shard)
    return jnp.stack([blocks, inside, earlier, further], axis=1).astype(jnp.int32)


def draw_qkv_weight(key, part):
    key = jax.random.fold_in(key, 37)
    base_key = jax.random.fold_in(key, 0)
    weights = jax.random.normal(base_key, (D, 3, D), jnp.float32) * D ** (-0.5)
    return jnp.clip(weights, -3.0, 3.0).astype(jnp.bfloat16)


def block_levels(key, extent, cuts, low, largest):
    gain = 1.0
    for position, shards_of in cuts:
        heights = jax.random.uniform(jax.random.fold_in(jax.random.fold_in(key, 6), position), (shards_of,), jnp.float32, low / len(cuts), largest / len(cuts))
        gain = gain * jnp.repeat(jnp.exp(heights), extent[position] // shards_of).reshape((-1,) + (1,) * (len(extent) - 1 - position))
    return gain


def bell_draw(key, dims, width, bound, cuts=(), held_as=jnp.bfloat16):
    loudness = block_levels(key, dims, cuts, -0.22, 0.18) if cuts else 1.0
    values = jax.random.normal(key, dims, jnp.float32) * width * loudness
    return jnp.minimum(jnp.maximum(values, -bound), bound).astype(held_as)


def setup_inputs(seed: int = 0) -> dict:
    splits = jax.random.split(jax.random.key(seed), 9)
    embeddings = bell_draw(splits[0], (TILES, EMB), 1.0, 6.0, ((0, 32),))
    positions = draw_positions(jax.random.fold_in(splits[8], 71), 0)
    in_weight = bell_draw(splits[2], (EMB, D), EMB ** -0.5, 0.15625)
    norm_gain = jnp.clip(1.0 + 0.18 * jax.random.normal(splits[3], (D,), jnp.float32), 0.1, 1.9)
    qkv_weight = draw_qkv_weight(jax.random.fold_in(splits[8], 71), 0)
    out_weight = bell_draw(splits[5], (D, D), HEAD ** -0.5, 0.875, ((0, 4),))
    neighbors = draw_neighbors(jax.random.fold_in(splits[8], 71), 0)
    upstream = bell_draw(splits[7], (SEQ, D), (SEQ ** -0.5), 0.125, ((0, 8),))
    return {"embeddings": embeddings, "positions": positions, "in_weight": in_weight, "norm_gain": norm_gain, "qkv_weight": qkv_weight, "out_weight": out_weight, "neighbors": neighbors, "upstream": upstream}


EPS = 1e-05

def as_rounded(values):
    return lax.optimization_barrier(values.astype(jnp.bfloat16)).astype(jnp.float32)

def attend_probs(queries, key_rows):
    num_blocks, block_rows, head_count, head_size = queries.shape
    scores = jnp.einsum('gqhd,gjkhd->ghqjk', queries.astype(jnp.float32), key_rows.astype(jnp.float32))
    scores = scores.reshape(num_blocks, head_count, block_rows, -1) * HEAD ** (-0.5)
    row_max = lax.optimization_barrier(jnp.max(scores, -1, keepdims=True))
    powers = jnp.exp(scores - row_max)
    row_sum = lax.optimization_barrier(jnp.sum(powers, -1, keepdims=True))
    return (powers / row_sum).astype(jnp.bfloat16)

def reference(embeddings, positions, in_weight, norm_gain, qkv_weight, out_weight, neighbors, upstream):
    kept_mask = positions >= 0
    target = jnp.where(kept_mask, positions, SEQ)
    slide_rows = jnp.zeros((SEQ, EMB), jnp.bfloat16).at[target].set(embeddings, mode='drop')
    start_x = jnp.dot(slide_rows, in_weight, preferred_element_type=jnp.float32).astype(jnp.bfloat16)
    x_float = start_x.astype(jnp.float32)
    centred = x_float - lax.optimization_barrier(jnp.mean(x_float, -1, keepdims=True))
    inv_std = lax.rsqrt(lax.optimization_barrier(jnp.mean(centred * centred, -1, keepdims=True)) + EPS)
    normed = centred * inv_std
    hidden = (normed * norm_gain).astype(jnp.bfloat16)
    project = jnp.dot(hidden, qkv_weight.reshape(D, 3 * D), preferred_element_type=jnp.float32)
    project = project.astype(jnp.bfloat16).reshape(SEQ, 3, D)
    head_count = D // HEAD
    blocks = project.reshape(NBLK, BLOCK, 3, head_count, HEAD)
    per_shard = SEQ_DEV // BLOCK
    groups = NBLK // per_shard

    def gather_group(index):
        block_list = lax.dynamic_slice_in_dim(neighbors, index * per_shard, per_shard, 0)
        queries = lax.dynamic_slice_in_dim(blocks, index * per_shard, per_shard, 0)[:, :, 0]
        chosen = blocks[block_list]
        return (block_list, queries, chosen[:, :, :, 1], chosen[:, :, :, 2])

    def forward_group(index):
        block_list, queries, key_rows, value_rows = gather_group(index)
        attn_probs = as_rounded(attend_probs(queries, key_rows))
        flat_values = value_rows.reshape(per_shard, NBR * BLOCK, head_count, HEAD).astype(jnp.float32)
        return jnp.einsum('ghqm,gmhd->gqhd', attn_probs, flat_values).astype(jnp.bfloat16)
    mixed = lax.map(forward_group, jnp.arange(groups, dtype=jnp.int32)).reshape(SEQ, D)
    group_cols = D // HEAD_GROUPS
    attn_total = jnp.zeros((SEQ, D), jnp.float32)
    for member in range(HEAD_GROUPS):
        piece = jnp.dot(mixed[:, member * group_cols:(member + 1) * group_cols], out_weight[member * group_cols:(member + 1) * group_cols], preferred_element_type=jnp.float32)
        attn_total = attn_total + as_rounded(piece)
    encoded = (x_float + attn_total).astype(jnp.bfloat16)
    d_mixed = lax.dot_general(upstream, out_weight, (((1,), (1,)), ((), ())), preferred_element_type=jnp.float32).astype(jnp.bfloat16)
    out_grad = lax.dot_general(mixed, upstream, (((0,), (0,)), ((), ())), preferred_element_type=jnp.float32)
    dout_blocks = d_mixed.reshape(NBLK, BLOCK, head_count, HEAD)

    def backward_group(carry, index):
        key_grad, value_grad = carry
        block_list, queries, key_rows, value_rows = gather_group(index)
        attn_probs = as_rounded(attend_probs(queries, key_rows))
        d_out = lax.dynamic_slice_in_dim(dout_blocks, index * per_shard, per_shard, 0).astype(jnp.float32)
        flat_keys = key_rows.reshape(per_shard, NBR * BLOCK, head_count, HEAD).astype(jnp.float32)
        flat_values = value_rows.reshape(per_shard, NBR * BLOCK, head_count, HEAD).astype(jnp.float32)
        prob_grad = jnp.einsum('gqhd,gmhd->ghqm', d_out, flat_values)
        row_dot = lax.optimization_barrier(jnp.sum(attn_probs * prob_grad, -1, keepdims=True))
        score_grad = as_rounded(attn_probs * (prob_grad - row_dot) * HEAD ** (-0.5))
        d_query = jnp.einsum('ghqm,gmhd->gqhd', score_grad, flat_keys).astype(jnp.bfloat16)
        d_key = jnp.einsum('ghqm,gqhd->gmhd', score_grad, queries.astype(jnp.float32))
        d_value = jnp.einsum('ghqm,gqhd->gmhd', attn_probs, d_out)
        key_grad = key_grad.at[block_list].add(d_key.reshape(per_shard, NBR, BLOCK, head_count, HEAD))
        value_grad = value_grad.at[block_list].add(d_value.reshape(per_shard, NBR, BLOCK, head_count, HEAD))
        return ((key_grad, value_grad), d_query)
    zero_grads = jnp.zeros((NBLK, BLOCK, head_count, HEAD), jnp.float32)
    (key_grad, value_grad), d_query = lax.scan(backward_group, (zero_grads, zero_grads), jnp.arange(groups, dtype=jnp.int32))
    d_project = jnp.stack([d_query.reshape(SEQ, D), key_grad.reshape(SEQ, D).astype(jnp.bfloat16), value_grad.reshape(SEQ, D).astype(jnp.bfloat16)], 1)
    qkv_grad = lax.dot_general(hidden, d_project.reshape(SEQ, 3 * D), (((0,), (0,)), ((), ())), preferred_element_type=jnp.float32).reshape(D, 3, D)
    d_hidden = jnp.zeros((SEQ, D), jnp.float32)
    for member in range(HEAD_GROUPS):
        grad_cols = d_project[:, :, member * group_cols:(member + 1) * group_cols].reshape(SEQ, 3 * group_cols)
        weight_cols = qkv_weight[:, :, member * group_cols:(member + 1) * group_cols].reshape(D, 3 * group_cols)
        piece = lax.dot_general(grad_cols, weight_cols, (((1,), (1,)), ((), ())), preferred_element_type=jnp.float32)
        d_hidden = d_hidden + as_rounded(piece)
    gain_grad = lax.optimization_barrier(jnp.sum(d_hidden * normed, 0))
    d_normed = d_hidden * norm_gain
    d_start = upstream.astype(jnp.float32) + inv_std * (d_normed - lax.optimization_barrier(jnp.mean(d_normed, -1, keepdims=True)) - normed * lax.optimization_barrier(jnp.mean(d_normed * normed, -1, keepdims=True)))
    d_start = d_start.astype(jnp.bfloat16)
    in_grad = lax.dot_general(slide_rows, d_start, (((0,), (0,)), ((), ())), preferred_element_type=jnp.float32)
    return (encoded, in_grad, gain_grad, qkv_grad, out_grad)
```

```python
import functools

import jax
import jax.numpy as jnp
from jax import lax
from jax.experimental import pallas as pl
from jax.experimental.pallas import tpu as pltpu
from jax.sharding import PartitionSpec as P

HEAD = 48
BLOCK = 128
NBR = 4
EPS = 1e-05
SCALE = HEAD ** (-0.5)
F32 = jnp.float32
BF16 = jnp.bfloat16
VMEM_BYTES = 52 * 1024 * 1024


def dot(a, b, ca, cb):
    return lax.dot_general(a, b, (((ca,), (cb,)), ((), ())), preferred_element_type=F32)


def params():
    return pltpu.CompilerParams(
        vmem_limit_bytes=VMEM_BYTES, dimension_semantics=("arbitrary",)
    )


def cost(flops, bytes_accessed, exps=0):
    return pl.CostEstimate(flops=flops, bytes_accessed=bytes_accessed, transcendentals=exps)


def centre(x):
    centred = x - jnp.mean(x, -1, keepdims=True)
    inv_std = lax.rsqrt(jnp.mean(centred * centred, -1, keepdims=True) + EPS)
    return centred * inv_std, inv_std


def project_kernel(x_ref, gain_ref, wt_ref, hidden_ref, q_ref, kv_ref):
    normed, _ = centre(x_ref[...].astype(F32))
    hidden = (normed * gain_ref[...]).astype(BF16)
    hidden_ref[...] = hidden
    cols = q_ref.shape[1]
    out = dot(wt_ref[...], hidden, 1, 1).astype(BF16)
    for g in range(q_ref.shape[0]):
        lanes = slice(g * BLOCK, (g + 1) * BLOCK)
        q_ref[g] = out[:cols, lanes]
        kv_ref[g] = out[cols:, lanes]


def project_rows(x, gain, wt, cols):
    rows, width = x.shape
    step = 4
    blocks = rows // BLOCK
    return pl.pallas_call(
        project_kernel,
        grid=(blocks // step,),
        in_specs=[
            pl.BlockSpec((step * BLOCK, width), lambda i: (i, 0)),
            pl.BlockSpec((1, width), lambda i: (0, 0)),
            pl.BlockSpec(wt.shape, lambda i: (0, 0)),
        ],
        out_specs=[
            pl.BlockSpec((step * BLOCK, width), lambda i: (i, 0)),
            pl.BlockSpec((step, cols, BLOCK), lambda i: (i, 0, 0)),
            pl.BlockSpec((step, 2 * cols, BLOCK), lambda i: (i, 0, 0)),
        ],
        out_shape=[
            jax.ShapeDtypeStruct((rows, width), BF16),
            jax.ShapeDtypeStruct((blocks, cols, BLOCK), BF16),
            jax.ShapeDtypeStruct((blocks, 2 * cols, BLOCK), BF16),
        ],
        compiler_params=params(),
        cost_estimate=cost(2 * rows * width * 3 * cols, 4 * rows * width + 8 * rows * cols),
    )(x, gain, wt)


def neighbour_rows(index_ref, kv_ref, low, high):
    b = pl.program_id(0)
    return jnp.concatenate(
        [kv_ref[index_ref[b * NBR + j], low:high, :] for j in range(NBR)], axis=1
    )


def forward_kernel(index_ref, q_ref, kv_ref, ow_ref, up_ref, part_ref, probs_ref, og_ref):
    cols = q_ref.shape[1]
    mixed = []
    for h in range(cols // HEAD):
        low, high = h * HEAD, (h + 1) * HEAD
        keys = neighbour_rows(index_ref, kv_ref, low, high)
        values = neighbour_rows(index_ref, kv_ref, cols + low, cols + high)
        scores = dot(q_ref[0, low:high, :], keys, 0, 0) * SCALE
        powers = jnp.exp(scores - jnp.max(scores, -1, keepdims=True))
        inverse = 1.0 / jnp.sum(powers, -1, keepdims=True)
        probs = (powers * inverse).astype(BF16)
        probs_ref[0, h] = probs
        mixed.append(dot(values, probs, 1, 1).astype(BF16))
    mixed = jnp.concatenate(mixed, axis=0)
    part_ref[...] = dot(mixed, ow_ref[...], 0, 0).astype(BF16)

    @pl.when(pl.program_id(0) == 0)
    def _():
        og_ref[...] = jnp.zeros_like(og_ref)

    og_ref[...] += dot(mixed, up_ref[...], 1, 0)


def attend_forward(index, q, kv, ow, up):
    blocks, cols, _ = q.shape
    rows, width = up.shape
    heads = cols // HEAD
    whole = lambda s: pl.BlockSpec(s, lambda i, r: (0,) * len(s))
    return pl.pallas_call(
        forward_kernel,
        grid_spec=pltpu.PrefetchScalarGridSpec(
            num_scalar_prefetch=1,
            grid=(blocks,),
            in_specs=[
                pl.BlockSpec((1, cols, BLOCK), lambda i, r: (i, 0, 0)),
                whole(kv.shape),
                whole(ow.shape),
                pl.BlockSpec((BLOCK, width), lambda i, r: (i, 0)),
            ],
            out_specs=[
                pl.BlockSpec((BLOCK, width), lambda i, r: (i, 0)),
                pl.BlockSpec((1, heads, BLOCK, NBR * BLOCK), lambda i, r: (i, 0, 0, 0)),
                whole(ow.shape),
            ],
        ),
        out_shape=[
            jax.ShapeDtypeStruct((rows, width), BF16),
            jax.ShapeDtypeStruct((blocks, heads, BLOCK, NBR * BLOCK), BF16),
            jax.ShapeDtypeStruct(ow.shape, F32),
        ],
        compiler_params=params(),
        cost_estimate=cost(
            16 * rows * cols * NBR * BLOCK, 40 * rows * width, rows * heads * NBR * BLOCK
        ),
    )(index, q, kv, ow, up)


def backward_kernel(
    index_ref, q_ref, kv_ref, ow_ref, up_ref, probs_ref,
    dq_ref, before_ref, own_ref, after_ref, total_ref,
):
    b = pl.program_id(0)
    cols = q_ref.shape[1]
    per_shard = own_ref.shape[0]

    @pl.when(b == 0)
    def _():
        @pl.loop(0, 3 * per_shard)
        def _(i):
            total_ref[i] = jnp.zeros(total_ref.shape[1:], F32)

    d_mixed = dot(ow_ref[...], up_ref[...], 1, 1).astype(BF16)
    key_terms, value_terms = [], []
    for h in range(cols // HEAD):
        low, high = h * HEAD, (h + 1) * HEAD
        keys = neighbour_rows(index_ref, kv_ref, low, high)
        values = neighbour_rows(index_ref, kv_ref, cols + low, cols + high)
        probs = probs_ref[0, h]
        d_out = d_mixed[low:high, :]
        prob_grad = dot(d_out, values, 0, 0)
        weight = probs.astype(F32)
        row_dot = jnp.sum(weight * prob_grad, -1, keepdims=True)
        score_grad = (weight * (prob_grad - row_dot) * SCALE).astype(BF16)
        dq_ref[0, low:high, :] = dot(keys, score_grad, 1, 1).astype(BF16)
        key_terms.append(dot(q_ref[0, low:high, :], score_grad, 1, 0))
        value_terms.append(dot(d_out, probs, 1, 0))
    terms = jnp.concatenate(key_terms + value_terms, axis=0)
    for j in range(NBR):
        total_ref[index_ref[b * NBR + j]] += terms[:, j * BLOCK : (j + 1) * BLOCK]

    @pl.when(b == per_shard - 1)
    def _():
        @pl.loop(0, per_shard)
        def _(i):
            before_ref[i] = total_ref[i].astype(BF16)
            own_ref[i] = total_ref[per_shard + i]
            after_ref[i] = total_ref[2 * per_shard + i].astype(BF16)


def attend_backward(index, q, kv, ow, up, probs):
    blocks, cols, _ = q.shape
    rows, width = up.shape
    heads = cols // HEAD
    whole = lambda s: pl.BlockSpec(s, lambda i, r: (0,) * len(s))
    grads = (blocks, 2 * cols, BLOCK)
    return pl.pallas_call(
        backward_kernel,
        grid_spec=pltpu.PrefetchScalarGridSpec(
            num_scalar_prefetch=1,
            grid=(blocks,),
            in_specs=[
                pl.BlockSpec((1, cols, BLOCK), lambda i, r: (i, 0, 0)),
                whole(kv.shape),
                whole(ow.shape),
                pl.BlockSpec((BLOCK, width), lambda i, r: (i, 0)),
                pl.BlockSpec((1, heads, BLOCK, NBR * BLOCK), lambda i, r: (i, 0, 0, 0)),
            ],
            out_specs=[
                pl.BlockSpec((1, cols, BLOCK), lambda i, r: (i, 0, 0)),
                whole(grads),
                whole(grads),
                whole(grads),
            ],
            scratch_shapes=[pltpu.VMEM((3 * blocks, 2 * cols, BLOCK), F32)],
        ),
        out_shape=[
            jax.ShapeDtypeStruct(q.shape, BF16),
            jax.ShapeDtypeStruct(grads, BF16),
            jax.ShapeDtypeStruct(grads, F32),
            jax.ShapeDtypeStruct(grads, BF16),
        ],
        compiler_params=params(),
        cost_estimate=cost(32 * rows * cols * NBR * BLOCK, 60 * rows * width),
    )(index, q, kv, ow, up, probs)


def product_kernel(dq_ref, own_ref, right_ref, left_ref, hid_ref, wt_ref, part_ref, qg_ref, dp_ref):
    i = pl.program_id(0)
    cols = dq_ref.shape[1]
    for g in range(dq_ref.shape[0]):
        lanes = slice(g * BLOCK, (g + 1) * BLOCK)
        dp_ref[:cols, lanes] = dq_ref[g]
        total = own_ref[g] + right_ref[g].astype(F32) + left_ref[g].astype(F32)
        dp_ref[cols:, lanes] = total.astype(BF16)
    dp = dp_ref[...]
    part_ref[...] = dot(dp, wt_ref[...], 0, 0).astype(BF16)

    @pl.when(i == 0)
    def _():
        qg_ref[...] = jnp.zeros_like(qg_ref)

    qg_ref[...] += dot(dp, hid_ref[...], 1, 0)


def gradient_products(dq, own, right, left, hidden, wt):
    blocks, cols, _ = dq.shape
    rows, width = hidden.shape
    step = 4
    side = pl.BlockSpec((step, 2 * cols, BLOCK), lambda i: (i, 0, 0))
    return pl.pallas_call(
        product_kernel,
        grid=(blocks // step,),
        in_specs=[
            pl.BlockSpec((step, cols, BLOCK), lambda i: (i, 0, 0)),
            side,
            side,
            side,
            pl.BlockSpec((step * BLOCK, width), lambda i: (i, 0)),
            pl.BlockSpec(wt.shape, lambda i: (0, 0)),
        ],
        out_specs=[
            pl.BlockSpec((step * BLOCK, width), lambda i: (i, 0)),
            pl.BlockSpec(wt.shape, lambda i: (0, 0)),
        ],
        out_shape=[
            jax.ShapeDtypeStruct((rows, width), BF16),
            jax.ShapeDtypeStruct(wt.shape, F32),
        ],
        scratch_shapes=[pltpu.VMEM((3 * cols, step * BLOCK), BF16)],
        compiler_params=params(),
        cost_estimate=cost(4 * rows * width * 3 * cols, 4 * rows * width + 18 * rows * cols),
    )(dq, own, right, left, hidden, wt)


def norm_back_kernel(dh_ref, x_ref, up_ref, gain_ref, ds_ref, gg_ref):
    normed, inv_std = centre(x_ref[...].astype(F32))
    d_hidden = dh_ref[...].astype(F32)
    grad = d_hidden * gain_ref[...]
    d_start = up_ref[...].astype(F32) + inv_std * (
        grad
        - jnp.mean(grad, -1, keepdims=True)
        - normed * jnp.mean(grad * normed, -1, keepdims=True)
    )
    ds_ref[...] = d_start.astype(BF16)

    @pl.when(pl.program_id(0) == 0)
    def _():
        gg_ref[...] = jnp.zeros_like(gg_ref)

    gg_ref[...] += jnp.sum(d_hidden * normed, 0, keepdims=True)


def norm_back(d_hidden, x, up, gain):
    rows, width = x.shape
    step = 4 * BLOCK
    tile = pl.BlockSpec((step, width), lambda i: (i, 0))
    line = pl.BlockSpec((1, width), lambda i: (0, 0))
    return pl.pallas_call(
        norm_back_kernel,
        grid=(rows // step,),
        in_specs=[tile, tile, tile, line],
        out_specs=[tile, line],
        out_shape=[
            jax.ShapeDtypeStruct((rows, width), BF16),
            jax.ShapeDtypeStruct((1, width), F32),
        ],
        compiler_params=params(),
        cost_estimate=cost(30 * rows * width, 8 * rows * width),
    )(d_hidden, x, up, gain)


def from_behind(value, axis, steps):
    count = lax.axis_size(axis)
    initial, last = (max(0, -steps), min(count, count - steps))
    return lax.ppermute(value, axis, [(source, source + steps) for source in range(initial, last)])


def mm(a, b):
    return jnp.dot(a, b, preferred_element_type=F32).astype(BF16)


def local(embeddings, positions, in_weight, norm_gain, qkv_weight, out_weight, neighbors, upstream):
    shards = lax.axis_size("ctx")
    my_shard = lax.axis_index("ctx")
    seq_dev, model_dim = upstream.shape
    per_shard = seq_dev // BLOCK
    produced = positions.shape[0]
    capacity = produced // shards
    cols = qkv_weight.shape[2]
    wt = qkv_weight.reshape(model_dim, 3 * cols).T
    gain = norm_gain.reshape(1, model_dim)

    target = jnp.floor_divide(positions, seq_dev)
    onehot = (target[:, None] == jnp.arange(shards, dtype=jnp.int32)[None, :]).astype(jnp.int32)
    order_in = jnp.sum((jnp.cumsum(onehot, 0) - onehot) * onehot, 1)
    slot_index = jnp.where(positions >= 0, target * capacity + order_in, produced)
    local_pos = positions - target * seq_dev
    slots = jnp.arange(produced, dtype=jnp.int32)
    in_slot = slots[:, None] == slot_index[None, :]
    send_pos = jnp.max(jnp.where(in_slot, local_pos[None, :], -1), 1)
    pick = in_slot.astype(BF16)
    send_proj = mm(pick, mm(embeddings, in_weight))
    swap = functools.partial(
        lax.all_to_all, axis_name="ctx", split_axis=0, concat_axis=0, tiled=True
    )
    got_pos = swap(send_pos.reshape(shards, capacity)).reshape(produced)
    got_proj = swap(send_proj.reshape(shards, capacity, -1)).reshape(produced, -1)
    send_rows, got_proj = lax.optimization_barrier((mm(pick, embeddings), got_proj))
    got_rows = swap(send_rows.reshape(shards, capacity, -1)).reshape(produced, -1)
    place = (got_pos[None, :] == jnp.arange(seq_dev, dtype=jnp.int32)[:, None]).astype(BF16)
    start_x = lax.psum(mm(place, got_proj), "src")
    slide = mm(place, got_rows)

    hidden, q, kv = project_rows(start_x, gain, wt, cols)
    ext_kv = jnp.concatenate(
        [from_behind(kv, "ctx", 1), kv, from_behind(kv, "ctx", -1)], axis=0
    )
    my_lists = lax.dynamic_slice_in_dim(neighbors, my_shard * per_shard, per_shard, 0)
    index = (my_lists - (my_shard - 1) * per_shard).reshape(-1)
    part, probs, out_part = attend_forward(index, q, ext_kv, out_weight, upstream)
    attn_total = lax.psum(part, "src")
    out_sum = lax.psum(out_part.astype(BF16), "ctx")
    dq, before, own, after = attend_backward(index, q, ext_kv, out_weight, upstream, probs)
    from_right = from_behind(before, "ctx", -1)
    from_left = from_behind(after, "ctx", 1)
    hidden_part, qkv_part = gradient_products(dq, own, from_right, from_left, hidden, wt)
    hidden_part, qkv_part, attn_total, out_sum = lax.optimization_barrier(
        (hidden_part, qkv_part, attn_total, out_sum)
    )
    encoded = (start_x.astype(F32) + attn_total.astype(F32)).astype(BF16)
    d_hidden = lax.psum(hidden_part, "src")
    qkv_sum = lax.psum(qkv_part.astype(BF16), "ctx")
    d_hidden, qkv_sum, slide = lax.optimization_barrier((d_hidden, qkv_sum, slide))
    d_start, gain_part = norm_back(d_hidden, start_x, upstream, gain)
    in_part = lax.dot_general(slide, d_start, (((0,), (0,)), ((), ())), preferred_element_type=F32)
    row_share = lax.psum_scatter(in_part.astype(BF16), "ctx", scatter_dimension=0, tiled=True)
    in_grad = lax.psum_scatter(row_share, "src", scatter_dimension=1, tiled=True)
    gain_sum = lax.psum(gain_part.astype(BF16), "ctx").reshape(model_dim)
    qkv_grad = qkv_sum.T.reshape(model_dim, 3, cols)
    return (
        encoded,
        in_grad.astype(F32),
        gain_sum.astype(F32),
        qkv_grad.astype(F32),
        out_sum.astype(F32),
    )


def solution(mesh):
    return jax.shard_map(
        local,
        mesh=mesh,
        in_specs=(
            P(("src", "ctx"), None),
            P(("src", "ctx")),
            P(),
            P(),
            P(None, None, "src"),
            P("src", None),
            P(),
            P("ctx", None),
        ),
        out_specs=(P("ctx", None), P("ctx", "src"), P(), P(None, None, "src"), P("src", None)),
        check_vma=False,
    )
```

```python
import jax
import jax.numpy as jnp
from jax import lax
from jax.experimental import pallas as pl
from jax.experimental.pallas import tpu as pltpu
from jax.sharding import PartitionSpec as P

HEAD = 48
BLOCK = 128
NBR = 4
EPS = 1e-05
SCALE = HEAD ** (-0.5)
F32 = jnp.float32
BF16 = jnp.bfloat16
VMEM_BYTES = 52 * 1024 * 1024


def dot(a, b, ca, cb):
    return lax.dot_general(a, b, (((ca,), (cb,)), ((), ())), preferred_element_type=F32)


def params():
    return pltpu.CompilerParams(
        vmem_limit_bytes=VMEM_BYTES, dimension_semantics=("arbitrary",)
    )


def cost(flops, bytes_accessed, exps=0):
    return pl.CostEstimate(flops=flops, bytes_accessed=bytes_accessed, transcendentals=exps)


def centre(x):
    centred = x - jnp.mean(x, -1, keepdims=True)
    inv_std = lax.rsqrt(jnp.mean(centred * centred, -1, keepdims=True) + EPS)
    return centred * inv_std, inv_std


def project_kernel(x_ref, gain_ref, wt_ref, hidden_ref, q_ref, kv_ref):
    normed, _ = centre(x_ref[...].astype(F32))
    hidden = (normed * gain_ref[...]).astype(BF16)
    hidden_ref[...] = hidden
    cols = q_ref.shape[1]
    out = dot(wt_ref[...], hidden, 1, 1).astype(BF16)
    for g in range(q_ref.shape[0]):
        lanes = slice(g * BLOCK, (g + 1) * BLOCK)
        q_ref[g] = out[:cols, lanes]
        kv_ref[g] = out[cols:, lanes]


def project_rows(x, gain, wt, cols):
    rows, width = x.shape
    step = 4
    blocks = rows // BLOCK
    return pl.pallas_call(
        project_kernel,
        grid=(blocks // step,),
        in_specs=[
            pl.BlockSpec((step * BLOCK, width), lambda i: (i, 0)),
            pl.BlockSpec((1, width), lambda i: (0, 0)),
            pl.BlockSpec(wt.shape, lambda i: (0, 0)),
        ],
        out_specs=[
            pl.BlockSpec((step * BLOCK, width), lambda i: (i, 0)),
            pl.BlockSpec((step, cols, BLOCK), lambda i: (i, 0, 0)),
            pl.BlockSpec((step, 2 * cols, BLOCK), lambda i: (i, 0, 0)),
        ],
        out_shape=[
            jax.ShapeDtypeStruct((rows, width), BF16),
            jax.ShapeDtypeStruct((blocks, cols, BLOCK), BF16),
            jax.ShapeDtypeStruct((blocks, 2 * cols, BLOCK), BF16),
        ],
        compiler_params=params(),
        cost_estimate=cost(2 * rows * width * 3 * cols, 4 * rows * width + 8 * rows * cols),
    )(x, gain, wt)


def neighbour_rows(index_ref, kv_ref, low, high):
    b = pl.program_id(0)
    return jnp.concatenate(
        [kv_ref[index_ref[b * NBR + j], low:high, :] for j in range(NBR)], axis=1
    )


def forward_kernel(index_ref, q_ref, kv_ref, ow_ref, up_ref, part_ref, probs_ref, og_ref):
    cols = q_ref.shape[1]
    mixed = []
    for h in range(cols // HEAD):
        low, high = h * HEAD, (h + 1) * HEAD
        keys = neighbour_rows(index_ref, kv_ref, low, high)
        values = neighbour_rows(index_ref, kv_ref, cols + low, cols + high)
        scores = dot(q_ref[0, low:high, :], keys, 0, 0) * SCALE
        powers = jnp.exp(scores - jnp.max(scores, -1, keepdims=True))
        inverse = 1.0 / jnp.sum(powers, -1, keepdims=True)
        probs = (powers * inverse).astype(BF16)
        probs_ref[0, h] = probs
        mixed.append(dot(values, probs, 1, 1).astype(BF16))
    mixed = jnp.concatenate(mixed, axis=0)
    part_ref[...] = dot(mixed, ow_ref[...], 0, 0).astype(BF16)

    @pl.when(pl.program_id(0) == 0)
    def _():
        og_ref[...] = jnp.zeros_like(og_ref)

    og_ref[...] += dot(mixed, up_ref[...], 1, 0)


def attend_forward(index, q, kv, ow, up):
    blocks, cols, _ = q.shape
    rows, width = up.shape
    heads = cols // HEAD
    whole = lambda s: pl.BlockSpec(s, lambda i, r: (0,) * len(s))
    return pl.pallas_call(
        forward_kernel,
        grid_spec=pltpu.PrefetchScalarGridSpec(
            num_scalar_prefetch=1,
            grid=(blocks,),
            in_specs=[
                pl.BlockSpec((1, cols, BLOCK), lambda i, r: (i, 0, 0)),
                whole(kv.shape),
                whole(ow.shape),
                pl.BlockSpec((BLOCK, width), lambda i, r: (i, 0)),
            ],
            out_specs=[
                pl.BlockSpec((BLOCK, width), lambda i, r: (i, 0)),
                pl.BlockSpec((1, heads, BLOCK, NBR * BLOCK), lambda i, r: (i, 0, 0, 0)),
                whole(ow.shape),
            ],
        ),
        out_shape=[
            jax.ShapeDtypeStruct((rows, width), BF16),
            jax.ShapeDtypeStruct((blocks, heads, BLOCK, NBR * BLOCK), BF16),
            jax.ShapeDtypeStruct(ow.shape, F32),
        ],
        compiler_params=params(),
        cost_estimate=cost(
            16 * rows * cols * NBR * BLOCK, 40 * rows * width, rows * heads * NBR * BLOCK
        ),
    )(index, q, kv, ow, up)


def backward_kernel(
    index_ref, q_ref, kv_ref, ow_ref, up_ref, probs_ref,
    dq_ref, before_ref, own_ref, after_ref, total_ref,
):
    b = pl.program_id(0)
    cols = q_ref.shape[1]
    per_shard = own_ref.shape[0]

    @pl.when(b == 0)
    def _():
        @pl.loop(0, 3 * per_shard)
        def _(i):
            total_ref[i] = jnp.zeros(total_ref.shape[1:], F32)

    d_mixed = dot(ow_ref[...], up_ref[...], 1, 1).astype(BF16)
    key_terms, value_terms = [], []
    for h in range(cols // HEAD):
        low, high = h * HEAD, (h + 1) * HEAD
        keys = neighbour_rows(index_ref, kv_ref, low, high)
        values = neighbour_rows(index_ref, kv_ref, cols + low, cols + high)
        probs = probs_ref[0, h]
        d_out = d_mixed[low:high, :]
        prob_grad = dot(d_out, values, 0, 0)
        weight = probs.astype(F32)
        row_dot = jnp.sum(weight * prob_grad, -1, keepdims=True)
        score_grad = (weight * (prob_grad - row_dot) * SCALE).astype(BF16)
        dq_ref[0, low:high, :] = dot(keys, score_grad, 1, 1).astype(BF16)
        key_terms.append(dot(q_ref[0, low:high, :], score_grad, 1, 0))
        value_terms.append(dot(d_out, probs, 1, 0))
    terms = jnp.concatenate(key_terms + value_terms, axis=0)
    for j in range(NBR):
        total_ref[index_ref[b * NBR + j]] += terms[:, j * BLOCK : (j + 1) * BLOCK]

    @pl.when(b == per_shard - 1)
    def _():
        @pl.loop(0, per_shard)
        def _(i):
            before_ref[i] = total_ref[i].astype(BF16)
            own_ref[i] = total_ref[per_shard + i]
            after_ref[i] = total_ref[2 * per_shard + i].astype(BF16)


def attend_backward(index, q, kv, ow, up, probs):
    blocks, cols, _ = q.shape
    rows, width = up.shape
    heads = cols // HEAD
    whole = lambda s: pl.BlockSpec(s, lambda i, r: (0,) * len(s))
    grads = (blocks, 2 * cols, BLOCK)
    return pl.pallas_call(
        backward_kernel,
        grid_spec=pltpu.PrefetchScalarGridSpec(
            num_scalar_prefetch=1,
            grid=(blocks,),
            in_specs=[
                pl.BlockSpec((1, cols, BLOCK), lambda i, r: (i, 0, 0)),
                whole(kv.shape),
                whole(ow.shape),
                pl.BlockSpec((BLOCK, width), lambda i, r: (i, 0)),
                pl.BlockSpec((1, heads, BLOCK, NBR * BLOCK), lambda i, r: (i, 0, 0, 0)),
            ],
            out_specs=[
                pl.BlockSpec((1, cols, BLOCK), lambda i, r: (i, 0, 0)),
                whole(grads),
                whole(grads),
                whole(grads),
            ],
            scratch_shapes=[pltpu.VMEM((3 * blocks, 2 * cols, BLOCK), F32)],
        ),
        out_shape=[
            jax.ShapeDtypeStruct(q.shape, BF16),
            jax.ShapeDtypeStruct(grads, BF16),
            jax.ShapeDtypeStruct(grads, F32),
            jax.ShapeDtypeStruct(grads, BF16),
        ],
        compiler_params=params(),
        cost_estimate=cost(32 * rows * cols * NBR * BLOCK, 60 * rows * width),
    )(index, q, kv, ow, up, probs)


def product_kernel(dq_ref, own_ref, right_ref, left_ref, hid_ref, wt_ref, part_ref, qg_ref, dp_ref):
    i = pl.program_id(0)
    cols = dq_ref.shape[1]
    for g in range(dq_ref.shape[0]):
        lanes = slice(g * BLOCK, (g + 1) * BLOCK)
        dp_ref[:cols, lanes] = dq_ref[g]
        total = own_ref[g] + right_ref[g].astype(F32) + left_ref[g].astype(F32)
        dp_ref[cols:, lanes] = total.astype(BF16)
    dp = dp_ref[...]
    part_ref[...] = dot(dp, wt_ref[...], 0, 0).astype(BF16)

    @pl.when(i == 0)
    def _():
        qg_ref[...] = jnp.zeros_like(qg_ref)

    qg_ref[...] += dot(dp, hid_ref[...], 1, 0)


def gradient_products(dq, own, right, left, hidden, wt):
    blocks, cols, _ = dq.shape
    rows, width = hidden.shape
    step = 4
    side = pl.BlockSpec((step, 2 * cols, BLOCK), lambda i: (i, 0, 0))
    return pl.pallas_call(
        product_kernel,
        grid=(blocks // step,),
        in_specs=[
            pl.BlockSpec((step, cols, BLOCK), lambda i: (i, 0, 0)),
            side,
            side,
            side,
            pl.BlockSpec((step * BLOCK, width), lambda i: (i, 0)),
            pl.BlockSpec(wt.shape, lambda i: (0, 0)),
        ],
        out_specs=[
            pl.BlockSpec((step * BLOCK, width), lambda i: (i, 0)),
            pl.BlockSpec(wt.shape, lambda i: (0, 0)),
        ],
        out_shape=[
            jax.ShapeDtypeStruct((rows, width), BF16),
            jax.ShapeDtypeStruct(wt.shape, F32),
        ],
        scratch_shapes=[pltpu.VMEM((3 * cols, step * BLOCK), BF16)],
        compiler_params=params(),
        cost_estimate=cost(4 * rows * width * 3 * cols, 4 * rows * width + 18 * rows * cols),
    )(dq, own, right, left, hidden, wt)


def norm_back_kernel(dh_ref, x_ref, up_ref, gain_ref, ds_ref, gg_ref):
    normed, inv_std = centre(x_ref[...].astype(F32))
    d_hidden = dh_ref[...].astype(F32)
    grad = d_hidden * gain_ref[...]
    d_start = up_ref[...].astype(F32) + inv_std * (
        grad
        - jnp.mean(grad, -1, keepdims=True)
        - normed * jnp.mean(grad * normed, -1, keepdims=True)
    )
    ds_ref[...] = d_start.astype(BF16)

    @pl.when(pl.program_id(0) == 0)
    def _():
        gg_ref[...] = jnp.zeros_like(gg_ref)

    gg_ref[...] += jnp.sum(d_hidden * normed, 0, keepdims=True)


def norm_back(d_hidden, x, up, gain):
    rows, width = x.shape
    step = 4 * BLOCK
    tile = pl.BlockSpec((step, width), lambda i: (i, 0))
    line = pl.BlockSpec((1, width), lambda i: (0, 0))
    return pl.pallas_call(
        norm_back_kernel,
        grid=(rows // step,),
        in_specs=[tile, tile, tile, line],
        out_specs=[tile, line],
        out_shape=[
            jax.ShapeDtypeStruct((rows, width), BF16),
            jax.ShapeDtypeStruct((1, width), F32),
        ],
        compiler_params=params(),
        cost_estimate=cost(30 * rows * width, 8 * rows * width),
    )(d_hidden, x, up, gain)


def from_behind(value, axis, steps):
    count = lax.axis_size(axis)
    initial, last = (max(0, -steps), min(count, count - steps))
    return lax.ppermute(value, axis, [(source, source + steps) for source in range(initial, last)])


def exchange(value, axis):
    return lax.all_to_all(value, axis, split_axis=0, concat_axis=0, tiled=True)


def sum_scatter(value, axis):
    count = lax.axis_size(axis)
    terms = exchange(value.astype(BF16).reshape(count, -1, value.shape[-1]), axis)
    return jnp.sum(terms.astype(F32), 0)


def sum_all(value, axis):
    count = lax.axis_size(axis)
    share = sum_scatter(value, axis).astype(BF16)
    return exchange(jnp.broadcast_to(share, (count,) + share.shape), axis).reshape(value.shape)


def mm(a, b):
    return jnp.dot(a, b, preferred_element_type=F32).astype(BF16)


def local(embeddings, positions, in_weight, norm_gain, qkv_weight, out_weight, neighbors, upstream):
    shards = lax.axis_size("ctx")
    my_shard = lax.axis_index("ctx")
    seq_dev, model_dim = upstream.shape
    per_shard = seq_dev // BLOCK
    produced = positions.shape[0]
    capacity = produced // shards
    cols = qkv_weight.shape[2]
    wt = qkv_weight.reshape(model_dim, 3 * cols).T
    gain = norm_gain.reshape(1, model_dim)

    target = jnp.floor_divide(positions, seq_dev)
    onehot = (target[:, None] == jnp.arange(shards, dtype=jnp.int32)[None, :]).astype(jnp.int32)
    order_in = jnp.sum((jnp.cumsum(onehot, 0) - onehot) * onehot, 1)
    slot_index = jnp.where(positions >= 0, target * capacity + order_in, produced)
    local_pos = positions - target * seq_dev
    slots = jnp.arange(produced, dtype=jnp.int32)
    in_slot = slots[:, None] == slot_index[None, :]
    send_pos = jnp.max(jnp.where(in_slot, local_pos[None, :], -1), 1)
    pick = in_slot.astype(BF16)
    send_proj = mm(pick, mm(embeddings, in_weight))
    got_pos = exchange(send_pos.reshape(shards, capacity), "ctx").reshape(produced)
    got_proj = exchange(send_proj.reshape(shards, capacity, -1), "ctx").reshape(produced, -1)
    send_rows, got_proj = lax.optimization_barrier((mm(pick, embeddings), got_proj))
    got_rows = exchange(send_rows.reshape(shards, capacity, -1), "ctx").reshape(produced, -1)
    place = (got_pos[None, :] == jnp.arange(seq_dev, dtype=jnp.int32)[:, None]).astype(BF16)
    start_x = lax.psum(mm(place, got_proj), "src")
    start_x, slide = lax.optimization_barrier((start_x, mm(place, got_rows)))

    hidden, q, kv = project_rows(start_x, gain, wt, cols)
    ext_kv = jnp.concatenate(
        [from_behind(kv, "ctx", 1), kv, from_behind(kv, "ctx", -1)], axis=0
    )
    my_lists = lax.dynamic_slice_in_dim(neighbors, my_shard * per_shard, per_shard, 0)
    index = (my_lists - (my_shard - 1) * per_shard).reshape(-1)
    part, probs, out_part = attend_forward(index, q, ext_kv, out_weight, upstream)
    attn_total = lax.psum(part, "src")
    dq, before, own, after = attend_backward(index, q, ext_kv, out_weight, upstream, probs)
    from_right = from_behind(before, "ctx", -1)
    from_left = from_behind(after, "ctx", 1)
    hidden_part, qkv_part = gradient_products(dq, own, from_right, from_left, hidden, wt)
    weight_part = jnp.concatenate([qkv_part, out_part], axis=0)
    hidden_part, attn_total = lax.optimization_barrier((hidden_part, attn_total))
    d_hidden = lax.psum(hidden_part, "src")
    encoded = (start_x.astype(F32) + attn_total.astype(F32)).astype(BF16)
    weight_sum = sum_all(weight_part, "ctx").astype(F32)
    qkv_grad = weight_sum[: 3 * cols].T.reshape(model_dim, 3, cols)
    out_grad = weight_sum[3 * cols :]
    d_hidden, qkv_grad, out_grad, encoded = lax.optimization_barrier(
        (d_hidden, qkv_grad, out_grad, encoded)
    )
    d_start, gain_part = norm_back(d_hidden, start_x, upstream, gain)
    gain_terms = exchange(jnp.broadcast_to(gain_part.astype(BF16), (shards, model_dim)), "ctx")
    gain_grad = jnp.sum(gain_terms.astype(F32), 0)
    in_part = lax.dot_general(slide, d_start, (((0,), (0,)), ((), ())), preferred_element_type=F32)
    row_share = sum_scatter(in_part, "ctx")
    sources = lax.axis_size("src")
    col_parts = jnp.moveaxis(row_share.reshape(row_share.shape[0], sources, -1), 1, 0)
    in_grad = sum_scatter(col_parts.reshape(-1, col_parts.shape[-1]), "src")
    return (encoded, in_grad, gain_grad, qkv_grad, out_grad)


def solution(mesh):
    return jax.shard_map(
        local,
        mesh=mesh,
        in_specs=(
            P(("src", "ctx"), None),
            P(("src", "ctx")),
            P(),
            P(),
            P(None, None, "src"),
            P("src", None),
            P(),
            P("ctx", None),
        ),
        out_specs=(P("ctx", None), P("ctx", "src"), P(), P(None, None, "src"), P("src", None)),
        check_vma=False,
    )
```

```python
import jax
import jax.numpy as jnp
from jax import lax
from jax.experimental import pallas as pl
from jax.experimental.pallas import tpu as pltpu
from jax.sharding import PartitionSpec as P

HEAD = 48
BLOCK = 128
NBR = 4
EPS = 1e-05
SCALE = HEAD ** (-0.5)
F32 = jnp.float32
BF16 = jnp.bfloat16
VMEM_BYTES = 52 * 1024 * 1024


def dot(a, b, ca, cb):
    return lax.dot_general(a, b, (((ca,), (cb,)), ((), ())), preferred_element_type=F32)


def params():
    return pltpu.CompilerParams(
        vmem_limit_bytes=VMEM_BYTES, dimension_semantics=("arbitrary",)
    )


def cost(flops, bytes_accessed, exps=0):
    return pl.CostEstimate(flops=flops, bytes_accessed=bytes_accessed, transcendentals=exps)


def centre(x):
    centred = x - jnp.mean(x, -1, keepdims=True)
    inv_std = lax.rsqrt(jnp.mean(centred * centred, -1, keepdims=True) + EPS)
    return centred * inv_std, inv_std


def project_kernel(x_ref, gain_ref, wt_ref, hidden_ref, q_ref, kv_ref):
    normed, _ = centre(x_ref[...].astype(F32))
    hidden = (normed * gain_ref[...]).astype(BF16)
    hidden_ref[...] = hidden
    cols = q_ref.shape[1]
    out = dot(wt_ref[...], hidden, 1, 1).astype(BF16)
    for g in range(q_ref.shape[0]):
        lanes = slice(g * BLOCK, (g + 1) * BLOCK)
        q_ref[g] = out[:cols, lanes]
        kv_ref[g] = out[cols:, lanes]


def project_rows(x, gain, wt, cols):
    rows, width = x.shape
    step = 4
    blocks = rows // BLOCK
    return pl.pallas_call(
        project_kernel,
        grid=(blocks // step,),
        in_specs=[
            pl.BlockSpec((step * BLOCK, width), lambda i: (i, 0)),
            pl.BlockSpec((1, width), lambda i: (0, 0)),
            pl.BlockSpec(wt.shape, lambda i: (0, 0)),
        ],
        out_specs=[
            pl.BlockSpec((step * BLOCK, width), lambda i: (i, 0)),
            pl.BlockSpec((step, cols, BLOCK), lambda i: (i, 0, 0)),
            pl.BlockSpec((step, 2 * cols, BLOCK), lambda i: (i, 0, 0)),
        ],
        out_shape=[
            jax.ShapeDtypeStruct((rows, width), BF16),
            jax.ShapeDtypeStruct((blocks, cols, BLOCK), BF16),
            jax.ShapeDtypeStruct((blocks, 2 * cols, BLOCK), BF16),
        ],
        compiler_params=params(),
        cost_estimate=cost(2 * rows * width * 3 * cols, 4 * rows * width + 8 * rows * cols),
    )(x, gain, wt)


def neighbour_rows(index_ref, kv_ref, low, high):
    b = pl.program_id(0)
    return jnp.concatenate(
        [kv_ref[index_ref[b * NBR + j], low:high, :] for j in range(NBR)], axis=1
    )


def forward_kernel(index_ref, q_ref, kv_ref, ow_ref, up_ref, part_ref, probs_ref, og_ref):
    cols = q_ref.shape[1]
    mixed = []
    for h in range(cols // HEAD):
        low, high = h * HEAD, (h + 1) * HEAD
        keys = neighbour_rows(index_ref, kv_ref, low, high)
        values = neighbour_rows(index_ref, kv_ref, cols + low, cols + high)
        scores = dot(q_ref[0, low:high, :], keys, 0, 0) * SCALE
        powers = jnp.exp(scores - jnp.max(scores, -1, keepdims=True))
        inverse = 1.0 / jnp.sum(powers, -1, keepdims=True)
        probs = (powers * inverse).astype(BF16)
        probs_ref[0, h] = probs
        mixed.append(dot(values, probs, 1, 1).astype(BF16))
    mixed = jnp.concatenate(mixed, axis=0)
    part_ref[...] = dot(mixed, ow_ref[...], 0, 0).astype(BF16)

    @pl.when(pl.program_id(0) == 0)
    def _():
        og_ref[...] = jnp.zeros_like(og_ref)

    og_ref[...] += dot(mixed, up_ref[...], 1, 0)


def attend_forward(index, q, kv, ow, up):
    blocks, cols, _ = q.shape
    rows, width = up.shape
    heads = cols // HEAD
    whole = lambda s: pl.BlockSpec(s, lambda i, r: (0,) * len(s))
    return pl.pallas_call(
        forward_kernel,
        grid_spec=pltpu.PrefetchScalarGridSpec(
            num_scalar_prefetch=1,
            grid=(blocks,),
            in_specs=[
                pl.BlockSpec((1, cols, BLOCK), lambda i, r: (i, 0, 0)),
                whole(kv.shape),
                whole(ow.shape),
                pl.BlockSpec((BLOCK, width), lambda i, r: (i, 0)),
            ],
            out_specs=[
                pl.BlockSpec((BLOCK, width), lambda i, r: (i, 0)),
                pl.BlockSpec((1, heads, BLOCK, NBR * BLOCK), lambda i, r: (i, 0, 0, 0)),
                whole(ow.shape),
            ],
        ),
        out_shape=[
            jax.ShapeDtypeStruct((rows, width), BF16),
            jax.ShapeDtypeStruct((blocks, heads, BLOCK, NBR * BLOCK), BF16),
            jax.ShapeDtypeStruct(ow.shape, F32),
        ],
        compiler_params=params(),
        cost_estimate=cost(
            16 * rows * cols * NBR * BLOCK, 40 * rows * width, rows * heads * NBR * BLOCK
        ),
    )(index, q, kv, ow, up)


def backward_kernel(
    index_ref, q_ref, kv_ref, ow_ref, up_ref, probs_ref,
    dq_ref, before_ref, own_ref, after_ref, total_ref,
):
    b = pl.program_id(0)
    cols = q_ref.shape[1]
    per_shard = own_ref.shape[0]

    @pl.when(b == 0)
    def _():
        @pl.loop(0, 3 * per_shard)
        def _(i):
            total_ref[i] = jnp.zeros(total_ref.shape[1:], F32)

    d_mixed = dot(ow_ref[...], up_ref[...], 1, 1).astype(BF16)
    key_terms, value_terms = [], []
    for h in range(cols // HEAD):
        low, high = h * HEAD, (h + 1) * HEAD
        keys = neighbour_rows(index_ref, kv_ref, low, high)
        values = neighbour_rows(index_ref, kv_ref, cols + low, cols + high)
        probs = probs_ref[0, h]
        d_out = d_mixed[low:high, :]
        prob_grad = dot(d_out, values, 0, 0)
        weight = probs.astype(F32)
        row_dot = jnp.sum(weight * prob_grad, -1, keepdims=True)
        score_grad = (weight * (prob_grad - row_dot) * SCALE).astype(BF16)
        dq_ref[0, low:high, :] = dot(keys, score_grad, 1, 1).astype(BF16)
        key_terms.append(dot(q_ref[0, low:high, :], score_grad, 1, 0))
        value_terms.append(dot(d_out, probs, 1, 0))
    terms = jnp.concatenate(key_terms + value_terms, axis=0)
    for j in range(NBR):
        total_ref[index_ref[b * NBR + j]] += terms[:, j * BLOCK : (j + 1) * BLOCK]

    @pl.when(b == per_shard - 1)
    def _():
        @pl.loop(0, per_shard)
        def _(i):
            before_ref[i] = total_ref[i].astype(BF16)
            own_ref[i] = total_ref[per_shard + i]
            after_ref[i] = total_ref[2 * per_shard + i].astype(BF16)


def attend_backward(index, q, kv, ow, up, probs):
    blocks, cols, _ = q.shape
    rows, width = up.shape
    heads = cols // HEAD
    whole = lambda s: pl.BlockSpec(s, lambda i, r: (0,) * len(s))
    grads = (blocks, 2 * cols, BLOCK)
    return pl.pallas_call(
        backward_kernel,
        grid_spec=pltpu.PrefetchScalarGridSpec(
            num_scalar_prefetch=1,
            grid=(blocks,),
            in_specs=[
                pl.BlockSpec((1, cols, BLOCK), lambda i, r: (i, 0, 0)),
                whole(kv.shape),
                whole(ow.shape),
                pl.BlockSpec((BLOCK, width), lambda i, r: (i, 0)),
                pl.BlockSpec((1, heads, BLOCK, NBR * BLOCK), lambda i, r: (i, 0, 0, 0)),
            ],
            out_specs=[
                pl.BlockSpec((1, cols, BLOCK), lambda i, r: (i, 0, 0)),
                whole(grads),
                whole(grads),
                whole(grads),
            ],
            scratch_shapes=[pltpu.VMEM((3 * blocks, 2 * cols, BLOCK), F32)],
        ),
        out_shape=[
            jax.ShapeDtypeStruct(q.shape, BF16),
            jax.ShapeDtypeStruct(grads, BF16),
            jax.ShapeDtypeStruct(grads, F32),
            jax.ShapeDtypeStruct(grads, BF16),
        ],
        compiler_params=params(),
        cost_estimate=cost(32 * rows * cols * NBR * BLOCK, 60 * rows * width),
    )(index, q, kv, ow, up, probs)


def product_kernel(dq_ref, own_ref, right_ref, left_ref, hid_ref, wt_ref, part_ref, qg_ref, dp_ref):
    i = pl.program_id(0)
    cols = dq_ref.shape[1]
    for g in range(dq_ref.shape[0]):
        lanes = slice(g * BLOCK, (g + 1) * BLOCK)
        dp_ref[:cols, lanes] = dq_ref[g]
        total = own_ref[g] + right_ref[g].astype(F32) + left_ref[g].astype(F32)
        dp_ref[cols:, lanes] = total.astype(BF16)
    dp = dp_ref[...]
    part_ref[...] = dot(dp, wt_ref[...], 0, 0).astype(BF16)

    @pl.when(i == 0)
    def _():
        qg_ref[...] = jnp.zeros_like(qg_ref)

    qg_ref[...] += dot(dp, hid_ref[...], 1, 0)


def gradient_products(dq, own, right, left, hidden, wt):
    blocks, cols, _ = dq.shape
    rows, width = hidden.shape
    step = 4
    side = pl.BlockSpec((step, 2 * cols, BLOCK), lambda i: (i, 0, 0))
    return pl.pallas_call(
        product_kernel,
        grid=(blocks // step,),
        in_specs=[
            pl.BlockSpec((step, cols, BLOCK), lambda i: (i, 0, 0)),
            side,
            side,
            side,
            pl.BlockSpec((step * BLOCK, width), lambda i: (i, 0)),
            pl.BlockSpec(wt.shape, lambda i: (0, 0)),
        ],
        out_specs=[
            pl.BlockSpec((step * BLOCK, width), lambda i: (i, 0)),
            pl.BlockSpec(wt.shape, lambda i: (0, 0)),
        ],
        out_shape=[
            jax.ShapeDtypeStruct((rows, width), BF16),
            jax.ShapeDtypeStruct(wt.shape, F32),
        ],
        scratch_shapes=[pltpu.VMEM((3 * cols, step * BLOCK), BF16)],
        compiler_params=params(),
        cost_estimate=cost(4 * rows * width * 3 * cols, 4 * rows * width + 18 * rows * cols),
    )(dq, own, right, left, hidden, wt)


def norm_back_kernel(dh_ref, x_ref, up_ref, gain_ref, ds_ref, gg_ref):
    normed, inv_std = centre(x_ref[...].astype(F32))
    d_hidden = dh_ref[...].astype(F32)
    grad = d_hidden * gain_ref[...]
    d_start = up_ref[...].astype(F32) + inv_std * (
        grad
        - jnp.mean(grad, -1, keepdims=True)
        - normed * jnp.mean(grad * normed, -1, keepdims=True)
    )
    ds_ref[...] = d_start.astype(BF16)

    @pl.when(pl.program_id(0) == 0)
    def _():
        gg_ref[...] = jnp.zeros_like(gg_ref)

    gg_ref[...] += jnp.sum(d_hidden * normed, 0, keepdims=True)


def norm_back(d_hidden, x, up, gain):
    rows, width = x.shape
    step = 4 * BLOCK
    tile = pl.BlockSpec((step, width), lambda i: (i, 0))
    line = pl.BlockSpec((1, width), lambda i: (0, 0))
    return pl.pallas_call(
        norm_back_kernel,
        grid=(rows // step,),
        in_specs=[tile, tile, tile, line],
        out_specs=[tile, line],
        out_shape=[
            jax.ShapeDtypeStruct((rows, width), BF16),
            jax.ShapeDtypeStruct((1, width), F32),
        ],
        compiler_params=params(),
        cost_estimate=cost(30 * rows * width, 8 * rows * width),
    )(d_hidden, x, up, gain)


def from_behind(value, axis, steps):
    count = lax.axis_size(axis)
    initial, last = (max(0, -steps), min(count, count - steps))
    return lax.ppermute(value, axis, [(source, source + steps) for source in range(initial, last)])


def exchange(value, axis):
    return lax.all_to_all(value, axis, split_axis=0, concat_axis=0, tiled=True)


def sum_scatter(value, axis):
    count = lax.axis_size(axis)
    terms = exchange(value.astype(BF16).reshape(count, -1, value.shape[-1]), axis)
    return jnp.sum(terms.astype(F32), 0)


def sum_all(value, axis):
    count = lax.axis_size(axis)
    share = sum_scatter(value, axis).astype(BF16)
    return exchange(jnp.broadcast_to(share, (count,) + share.shape), axis).reshape(value.shape)


def mm(a, b):
    return jnp.dot(a, b, preferred_element_type=F32).astype(BF16)


def local(embeddings, positions, in_weight, norm_gain, qkv_weight, out_weight, neighbors, upstream):
    shards = lax.axis_size("ctx")
    my_shard = lax.axis_index("ctx")
    seq_dev, model_dim = upstream.shape
    per_shard = seq_dev // BLOCK
    produced = positions.shape[0]
    capacity = produced // shards
    cols = qkv_weight.shape[2]
    wt = qkv_weight.reshape(model_dim, 3 * cols).T
    gain = norm_gain.reshape(1, model_dim)

    target = jnp.floor_divide(positions, seq_dev)
    onehot = (target[:, None] == jnp.arange(shards, dtype=jnp.int32)[None, :]).astype(jnp.int32)
    order_in = jnp.sum((jnp.cumsum(onehot, 0) - onehot) * onehot, 1)
    slot_index = jnp.where(positions >= 0, target * capacity + order_in, produced)
    local_pos = positions - target * seq_dev
    slots = jnp.arange(produced, dtype=jnp.int32)
    in_slot = slots[:, None] == slot_index[None, :]
    send_pos = jnp.max(jnp.where(in_slot, local_pos[None, :], -1), 1)
    pick = in_slot.astype(BF16)
    send_proj = mm(pick, mm(embeddings, in_weight))
    got_pos = exchange(send_pos.reshape(shards, capacity), "ctx").reshape(produced)
    got_proj = exchange(send_proj.reshape(shards, capacity, -1), "ctx").reshape(produced, -1)
    send_rows, got_proj = lax.optimization_barrier((mm(pick, embeddings), got_proj))
    got_rows = exchange(send_rows.reshape(shards, capacity, -1), "ctx").reshape(produced, -1)
    half = seq_dev // 2
    rows_low = jnp.arange(half, dtype=jnp.int32)[:, None]
    place_low = (got_pos[None, :] == rows_low).astype(BF16)
    place_high = (got_pos[None, :] == rows_low + half).astype(BF16)
    x_low = lax.psum(mm(place_low, got_proj), "src")
    placed_high, x_low = lax.optimization_barrier((mm(place_high, got_proj), x_low))
    x_high = lax.psum(placed_high, "src")
    hidden_low, q_low, kv_low = project_rows(x_low, gain, wt, cols)
    left_low = from_behind(kv_low, "ctx", 1)
    right_low = from_behind(kv_low, "ctx", -1)
    place = jnp.concatenate([place_low, place_high], axis=0)
    x_high, slide, left_low, right_low = lax.optimization_barrier(
        (x_high, mm(place, got_rows), left_low, right_low)
    )
    hidden_high, q_high, kv_high = project_rows(x_high, gain, wt, cols)
    ext_kv = jnp.concatenate(
        [
            left_low,
            from_behind(kv_high, "ctx", 1),
            kv_low,
            kv_high,
            right_low,
            from_behind(kv_high, "ctx", -1),
        ],
        axis=0,
    )
    q = jnp.concatenate([q_low, q_high], axis=0)
    hidden = jnp.concatenate([hidden_low, hidden_high], axis=0)
    start_x = jnp.concatenate([x_low, x_high], axis=0)
    my_lists = lax.dynamic_slice_in_dim(neighbors, my_shard * per_shard, per_shard, 0)
    index = (my_lists - (my_shard - 1) * per_shard).reshape(-1)
    part, probs, out_part = attend_forward(index, q, ext_kv, out_weight, upstream)
    attn_total = lax.psum(part, "src")
    dq, before, own, after = attend_backward(index, q, ext_kv, out_weight, upstream, probs)
    from_right = from_behind(before, "ctx", -1)
    from_left = from_behind(after, "ctx", 1)
    hidden_part, qkv_part = gradient_products(dq, own, from_right, from_left, hidden, wt)
    weight_part = jnp.concatenate([qkv_part, out_part], axis=0)
    hidden_part, attn_total = lax.optimization_barrier((hidden_part, attn_total))
    d_hidden = lax.psum(hidden_part, "src")
    encoded = (start_x.astype(F32) + attn_total.astype(F32)).astype(BF16)
    weight_sum = sum_all(weight_part, "ctx").astype(F32)
    qkv_grad = weight_sum[: 3 * cols].T.reshape(model_dim, 3, cols)
    out_grad = weight_sum[3 * cols :]
    d_hidden, qkv_grad, out_grad, encoded = lax.optimization_barrier(
        (d_hidden, qkv_grad, out_grad, encoded)
    )
    d_start, gain_part = norm_back(d_hidden, start_x, upstream, gain)
    gain_terms = exchange(jnp.broadcast_to(gain_part.astype(BF16), (shards, model_dim)), "ctx")
    in_part = dot(slide, d_start, 0, 0).astype(BF16)
    in_part, gain_terms = lax.optimization_barrier((in_part, gain_terms))
    row_share = sum_scatter(in_part, "ctx")
    gain_grad = jnp.sum(gain_terms.astype(F32), 0)
    sources = lax.axis_size("src")
    col_parts = jnp.moveaxis(row_share.reshape(row_share.shape[0], sources, -1), 1, 0)
    in_grad = sum_scatter(col_parts.reshape(-1, col_parts.shape[-1]), "src")
    return (encoded, in_grad, gain_grad, qkv_grad, out_grad)


def solution(mesh):
    return jax.shard_map(
        local,
        mesh=mesh,
        in_specs=(
            P(("src", "ctx"), None),
            P(("src", "ctx")),
            P(),
            P(),
            P(None, None, "src"),
            P("src", None),
            P(),
            P("ctx", None),
        ),
        out_specs=(P("ctx", None), P("ctx", "src"), P(), P(None, None, "src"), P("src", None)),
        check_vma=False,
    )
```
